32 devices in a mesh: patch: 4 (over z), seq: 4 (over y, x), cfg: 2 (over core).
Axes of the slice: x: 2, y: 2, z: 4, core: 2. Of those that a mesh axis runs over, the one named last changes fastest.
Arguments:
- query: bfloat16 [18432, 2048], P(('cfg', 'patch', 'seq')), parts along dimension 0, may hold values from -16 to 16
- fresh_key: bfloat16 [18432, 2048], P(('cfg', 'patch', 'seq')), parts along dimension 0, may hold values from -6 to 6
- fresh_value: bfloat16 [18432, 2048], P(('cfg', 'patch', 'seq')), parts along dimension 0, may hold values from -6 to 6
- stale_key: bfloat16 [18432, 2048], P(('cfg', 'patch', 'seq')), parts along dimension 0, may hold values from -6 to 6
- stale_value: bfloat16 [18432, 2048], P(('cfg', 'patch', 'seq')), parts along dimension 0, may hold values from -6 to 6
- key_tiles: int32 [24, 18], P('patch'), may hold values from 0 to 23, as said below
- tile_count: int32 [24], P('patch'), may hold values from 1 to 18
Outputs:
- attended: bfloat16 [18432, 2048], P(('cfg', 'patch', 'seq')), parts along dimension 0
The draws below stay inside these ranges and needn't reach their ends.
There are 2 independent parts, one for each index of `cfg`. The reference program is written for one: setup_inputs(seed, part) draws one part's arguments, and reference() takes and returns one part's arrays. A program takes and returns all parts, laid end to end along the dimension named above; an argument that names none is the same for every part. Nothing has to cross between parts.
Inputs may be any that keep to these rules, and one draw needn't show every extreme that they name: `key_tiles`: tile numbers are patch * 2 * 3 + row * 3 + column. The first tile_count[t] entries of row t are distinct tiles within one tile of t in patch, row and column (t itself among them); the other entries equal t and are ignored.
All inputs are finite; a program needn't handle non-finite values.
Results may differ from the reference program's by a relative error of at most 0.0049.
Values may be sent and summed in bfloat16 or wider, within the bound.
A program may use at most 128 MiB of HBM per device.

```python
import jax
import jax.numpy as jnp
import numpy as np
from jax import lax

NUM_HEADS = 16
HEAD_DIM = 128
TILE_TOKENS = 384
TILES_H = 2
TILES_W = 3
KEY_SLOTS = 18
TOKENS = 9216
ALL_TILES = 24


neighbour_table = np.array([[a, b, c] for a in (-1, 0, 1) for b in (-1, 0, 1) for c in (-1, 0, 1)], dtype=np.int32)


def tile_lists(key):
    per_patch = TILES_H * TILES_W
    patches = ALL_TILES // per_patch
    tiles = jnp.arange(ALL_TILES, dtype=jnp.int32)
    patch_of = tiles // per_patch
    rest = tiles % per_patch
    row_of = rest // TILES_W
    col_of = rest % TILES_W
    offsets = jnp.asarray(neighbour_table)
    near_patch = patch_of[:, None] + offsets[None, :, 0]
    near_row = row_of[:, None] + offsets[None, :, 1]
    near_col = col_of[:, None] + offsets[None, :, 2]
    inside = (near_patch >= 0) & (near_patch < patches) & (near_row >= 0) & (near_row < TILES_H) & (near_col >= 0) & (near_col < TILES_W)
    candidate = near_patch * per_patch + near_row * TILES_W + near_col
    coins = jax.random.randint(jax.random.fold_in(key, 11), (ALL_TILES, 27), 0, 4) > 0
    center = (offsets[:, 0] == 0) & (offsets[:, 1] == 0) & (offsets[:, 2] == 0)
    forced_tile = per_patch + min(1, TILES_H - 1) * TILES_W + min(1, TILES_W - 1)
    keep = inside & (coins | center[None, :] | (tiles == forced_tile)[:, None])
    noise = jax.random.randint(jax.random.fold_in(key, 12), (ALL_TILES, 27), 0, 65536)
    score = jnp.where(keep, 0, 1 << 22) + noise * 32 + jnp.arange(27, dtype=jnp.int32)[None, :]
    order = jnp.argsort(score, axis=1)[:, :KEY_SLOTS]
    picked = jnp.take_along_axis(candidate, order, axis=1)
    count = jnp.sum(keep.astype(jnp.int32), axis=1).astype(jnp.int32)
    slot = jnp.arange(KEY_SLOTS, dtype=jnp.int32)
    listed = jnp.where(slot[None, :] < count[:, None], picked, tiles[:, None])
    return (listed.astype(jnp.int32), count)


def draw_key_tiles(key, part):
    return tile_lists(key)[0]


def draw_tile_count(key, part):
    return tile_lists(key)[1]


def steps_of(stream_key, dims, split, smallest, largest):
    def one(dim, shards_of):
        draws = jax.random.uniform(jax.random.fold_in(jax.random.fold_in(stream_key, 6), dim), (shards_of,), jnp.float32, smallest / len(split), largest / len(split))
        return jnp.repeat(jnp.exp(draws), dims[dim] // shards_of).reshape((-1,) + (1,) * (len(dims) - dim - 1))

    level = one(*split[0])
    for cut in split[1:]:
        level = level * one(*cut)
    return level


def gaussian(own_key, extent, deviation, most, pieces=(), kind=jnp.bfloat16):
    entries = deviation * jax.random.normal(own_key, extent, jnp.float32)
    if pieces:
        entries = entries * steps_of(own_key, extent, pieces, -0.22, 0.18)
    return jnp.clip(entries, -most, most).astype(kind)


def setup_inputs(seed: int = 0, part: int = 0) -> dict:
    arg_keys = jax.random.split(jax.random.key(seed), 8)
    part_splits = jax.random.split(jax.random.fold_in(arg_keys[7], part), 8)
    return {
        "query": gaussian(part_splits[0], (TOKENS, NUM_HEADS * HEAD_DIM), 4.0, 16.0, ((0, 16),)),
        "fresh_key": gaussian(part_splits[1], (TOKENS, NUM_HEADS * HEAD_DIM), 1.0, 6.0, ((0, 16),)),
        "fresh_value": gaussian(part_splits[2], (TOKENS, NUM_HEADS * HEAD_DIM), 1.0, 6.0, ((0, 16),)),
        "stale_key": gaussian(part_splits[3], (TOKENS, NUM_HEADS * HEAD_DIM), 1.0, 6.0, ((0, 16),)),
        "stale_value": gaussian(part_splits[4], (TOKENS, NUM_HEADS * HEAD_DIM), 1.0, 6.0, ((0, 16),)),
        "key_tiles": draw_key_tiles(jax.random.fold_in(arg_keys[7], 71), part),
        "tile_count": draw_tile_count(jax.random.fold_in(arg_keys[7], 71), part),
    }


soft_cap = 8.0


def reference(query, fresh_key, fresh_value, stale_key, stale_value, key_tiles, tile_count):
    per_patch = TILES_H * TILES_W
    scale = 1.0 / (HEAD_DIM ** 0.5)

    def as_tiles(array):
        return array.reshape(ALL_TILES, TILE_TOKENS, NUM_HEADS, HEAD_DIM)

    query_t = as_tiles(query)
    fresh_k = as_tiles(fresh_key)
    fresh_v = as_tiles(fresh_value)
    stale_k = as_tiles(stale_key)
    stale_v = as_tiles(stale_value)

    def one_tile(index):
        listed = key_tiles[index].astype(jnp.int32)
        count = tile_count[index]
        same = (listed // per_patch) == (index // per_patch)
        keys = jnp.where(same[:, None, None, None], fresh_k[listed], stale_k[listed])
        values = jnp.where(same[:, None, None, None], fresh_v[listed], stale_v[listed])
        scores = jnp.einsum("qhd,sthd->hqst", query_t[index].astype(jnp.float32), keys.astype(jnp.float32)) * scale
        capped = soft_cap * jnp.tanh(scores / soft_cap)
        valid = jnp.arange(KEY_SLOTS, dtype=jnp.int32) < count
        weight = jnp.where(valid[None, None, :, None], jnp.exp(capped - soft_cap), jnp.float32(0.0))
        total = jnp.sum(weight, axis=(2, 3))
        weight_b = lax.optimization_barrier(weight.astype(jnp.bfloat16))
        numer = jnp.einsum("hqst,sthd->qhd", weight_b.astype(jnp.float32), values.astype(jnp.float32))
        return (numer / jnp.transpose(total)[:, :, None]).astype(jnp.bfloat16)

    result = lax.map(one_tile, jnp.arange(ALL_TILES, dtype=jnp.int32))
    return result.reshape(TOKENS, NUM_HEADS * HEAD_DIM)
```

```python
import functools
import math

import jax
import jax.numpy as jnp
from jax import lax
from jax.experimental import pallas as pl
from jax.experimental.pallas import tpu as pltpu
from jax.sharding import PartitionSpec as P

NUM_HEADS = 16
HEAD_DIM = 128
TILE_TOKENS = 384
TILES_H = 2
TILES_W = 3
KEY_SLOTS = 18
PER_PATCH = TILES_H * TILES_W

SOFT_CAP = 8.0
LOG2E = math.log2(math.e)
SCORE_SCALE = 1.0 / (SOFT_CAP * HEAD_DIM**0.5)
EXP_SCALE = SOFT_CAP * LOG2E
UNUSED = 1e30

MESH = pl.DeviceIdType.MESH
BEFORE, OWN, AFTER = 0, 1, 2
STALE, CURRENT = (0, 1), (2, 3, 4)


def kernel(
    seq_count, patch_count, rows, bias, query, fresh_key, fresh_value, stale_key, stale_value, out,
    q_buf, k_buf, v_buf, ks_buf, vs_buf, acc, o_buf,
    send_in, recv_in, send_z, recv_z, send_o, recv_o,
):
    heads = NUM_HEADS // seq_count
    row_devices = seq_count // TILES_H
    me = lax.axis_index("seq")
    patch = lax.axis_index("patch")
    has_before = patch > 0
    has_after = patch < patch_count - 1

    def peer_of(step):
        return lax.rem(me + step, seq_count)

    def columns(device, head):
        return pl.ds(pl.multiple_of((device * heads + head) * HEAD_DIM, HEAD_DIM), HEAD_DIM)

    def rows_of(device):
        return pl.ds(pl.multiple_of(device * rows, 16), rows)

    barrier = pltpu.get_barrier_semaphore()
    for step in range(1, seq_count):
        pl.semaphore_signal(barrier, inc=1, device_id={"seq": peer_of(step)}, device_id_type=MESH)

    @pl.when(has_before)
    def _():
        pl.semaphore_signal(barrier, inc=1, device_id={"patch": patch - 1}, device_id_type=MESH)

    @pl.when(has_after)
    def _():
        pl.semaphore_signal(barrier, inc=1, device_id={"patch": patch + 1}, device_id_type=MESH)

    around = jnp.minimum(patch, 1) + jnp.minimum(patch_count - 1 - patch, 1)
    pl.semaphore_wait(barrier, seq_count - 1 + around)

    sources = (stale_key, stale_value, query, fresh_key, fresh_value)

    def landing(array, head):
        return (
            ks_buf.at[head], vs_buf.at[head], q_buf.at[head], k_buf.at[OWN, head], v_buf.at[OWN, head]
        )[array]

    def send_inputs(arrays, head):
        for array in arrays:
            source = sources[array]
            for step in range(1, seq_count):
                peer = peer_of(step)
                pltpu.make_async_remote_copy(
                    src_ref=source.at[:, columns(peer, head)],
                    dst_ref=landing(array, head).at[rows_of(me)],
                    send_sem=send_in.at[array, head],
                    recv_sem=recv_in.at[array, head],
                    device_id={"seq": peer},
                    device_id_type=MESH,
                ).start()
            pltpu.make_async_copy(
                source.at[:, columns(me, head)],
                landing(array, head).at[rows_of(me)],
                recv_in.at[array, head],
            ).start()

    def wait_inputs(arrays, head):
        for array in arrays:
            whole = landing(array, head)
            pltpu.make_async_copy(whole, whole, recv_in.at[array, head]).wait()

    def halo_copy(array, side, head):
        source = (ks_buf, vs_buf)[array]
        target = (k_buf, v_buf)[array]
        return pltpu.make_async_remote_copy(
            src_ref=source.at[head],
            dst_ref=target.at[side, head],
            send_sem=send_z.at[array, side, head],
            recv_sem=recv_z.at[array, side, head],
            device_id={"patch": patch + 1 if side == BEFORE else patch - 1},
            device_id_type=MESH,
        )

    def send_halo(head):
        wait_inputs(STALE, head)
        for array in STALE:

            @pl.when(has_after)
            def _():
                halo_copy(array, BEFORE, head).start()

            @pl.when(has_before)
            def _():
                halo_copy(array, AFTER, head).start()

    def attend(head, side, row):
        ones = jnp.ones((2 * TILE_TOKENS, HEAD_DIM), jnp.bfloat16)
        steps = [
            (col, first)
            for col in range(TILES_W)
            for first in ((0, 2, 4) if col == 1 else (min(col, 1), TILES_W + min(col, 1)))
        ]

        def scores_of(col, first):
            start = (row * TILES_W + col) * TILE_TOKENS
            query_rows = q_buf[head, pl.ds(pl.multiple_of(start, TILE_TOKENS), TILE_TOKENS), :]
            return lax.dot_general(
                query_rows, k_buf[side, head, pl.ds(first * TILE_TOKENS, 2 * TILE_TOKENS), :],
                (((1,), (1,)), ((), ())), preferred_element_type=jnp.float32,
            )

        ahead = scores_of(*steps[0])
        partial = None
        for index, (col, first) in enumerate(steps):
            tile = row * TILES_W + col
            scores = ahead
            if index + 1 < len(steps):
                ahead = scores_of(*steps[index + 1])
            weights = []
            for part in range(2):
                shift = bias[tile, side * PER_PATCH + first + part]
                part_scores = scores[:, part * TILE_TOKENS : (part + 1) * TILE_TOKENS]
                weight = jnp.exp2(EXP_SCALE * jnp.tanh(part_scores * SCORE_SCALE) - shift)
                weights.append(weight.astype(jnp.bfloat16))
            at = pl.ds(first * TILE_TOKENS, 2 * TILE_TOKENS)
            values = jnp.concatenate([v_buf[side, head, at, :], ones], axis=1)
            term = jnp.dot(
                jnp.concatenate(weights, axis=1), values, preferred_element_type=jnp.float32
            )
            partial = term if partial is None else partial + term
            if index + 1 == len(steps) or steps[index + 1][0] != col:
                acc[tile] += partial
                partial = None

    def send_output(head, row):
        for step in range(1, seq_count):
            peer = peer_of(step)

            @pl.when(lax.div(peer, row_devices) == row)
            def _():
                pltpu.make_async_remote_copy(
                    src_ref=o_buf.at[head, rows_of(peer)],
                    dst_ref=out.at[:, columns(me, head)],
                    send_sem=send_o.at[head],
                    recv_sem=recv_o.at[head],
                    device_id={"seq": peer},
                    device_id_type=MESH,
                ).start()

        @pl.when(lax.div(me, row_devices) == row)
        def _():
            pltpu.make_async_copy(
                o_buf.at[head, rows_of(me)], out.at[:, columns(me, head)], recv_o.at[head]
            ).start()

    for head in range(min(2, heads)):
        send_inputs(STALE, head)
    send_halo(0)
    send_inputs(CURRENT, 0)
    if heads > 1:
        send_halo(1)
    if heads > 2:
        send_inputs(STALE, 2)

    def wait_halo(side, head):
        for array, target in enumerate((k_buf, v_buf)):
            whole = target.at[side, head]
            pltpu.make_async_copy(whole, whole, recv_z.at[array, side, head]).wait()

    def head_step(head, carry):
        acc[...] = jnp.zeros_like(acc)
        wait_inputs((2,), head)

        @pl.when(head + 1 < heads)
        def _():
            send_inputs(CURRENT, head + 1)

        def near_step(index, carry):
            side = 2 * index
            other = patch - 1 + side

            @pl.when(jnp.logical_and(other >= 0, other < patch_count))
            def _():
                wait_halo(side, head)

                def row_step(row, carry):
                    attend(head, side, row)
                    return carry

                lax.fori_loop(0, TILES_H, row_step, 0)

            return carry

        lax.fori_loop(0, 2, near_step, 0)
        wait_inputs((3, 4), head)

        def own_step(row, carry):
            attend(head, OWN, row)
            for col in range(TILES_W):
                tile = row * TILES_W + col
                tile_rows = pl.ds(pl.multiple_of(tile * TILE_TOKENS, TILE_TOKENS), TILE_TOKENS)
                o_buf[head, tile_rows, :] = (
                    acc[tile, :, :HEAD_DIM] / acc[tile, :, HEAD_DIM:]
                ).astype(jnp.bfloat16)
            send_output(head, row)
            return carry

        lax.fori_loop(0, TILES_H, own_step, 0)

        @pl.when(head + 2 < heads)
        def _():
            send_halo(head + 2)

        @pl.when(head + 3 < heads)
        def _():
            send_inputs(STALE, head + 3)

        return carry

    lax.fori_loop(0, heads, head_step, 0)

    sent = pl.ds(0, (seq_count - 1) * rows)
    for head in range(heads):
        for array in range(len(sources)):
            part = landing(array, head).at[sent]
            pltpu.make_async_copy(part, part, send_in.at[array, head]).wait()
        for array in STALE:

            @pl.when(has_after)
            def _():
                halo_copy(array, BEFORE, head).wait_send()

            @pl.when(has_before)
            def _():
                halo_copy(array, AFTER, head).wait_send()

        part = o_buf.at[head, sent]
        pltpu.make_async_copy(part, part, send_o.at[head]).wait()
        whole = o_buf.at[head]
        pltpu.make_async_copy(whole, whole, recv_o.at[head]).wait()


def on_device(query, fresh_key, fresh_value, stale_key, stale_value, key_tiles, tile_count):
    seq_count = lax.axis_size("seq")
    patch_count = lax.axis_size("patch")
    heads = NUM_HEADS // seq_count
    rows = query.shape[0]
    patch_rows = rows * seq_count
    first_tile = (lax.axis_index("patch") - 1) * PER_PATCH
    used = jnp.arange(KEY_SLOTS, dtype=jnp.int32)[None, :] < tile_count[:, None]
    near = jnp.arange(3 * PER_PATCH, dtype=jnp.int32)
    listed = jnp.any(
        used[:, :, None] & ((key_tiles - first_tile)[:, :, None] == near[None, None, :]), axis=1
    )
    bias = jnp.where(listed, EXP_SCALE, UNUSED).astype(jnp.float32)
    block = (heads, patch_rows, HEAD_DIM)
    pairs = patch_rows * TILES_H * 7 * TILE_TOKENS * 3 * heads // TILES_W
    return pl.pallas_call(
        functools.partial(kernel, seq_count, patch_count, rows),
        out_shape=jax.ShapeDtypeStruct(query.shape, jnp.bfloat16),
        in_specs=[pl.BlockSpec(memory_space=pltpu.SMEM)] + [pl.BlockSpec(memory_space=pl.ANY)] * 5,
        out_specs=pl.BlockSpec(memory_space=pl.ANY),
        scratch_shapes=[
            pltpu.VMEM(block, jnp.bfloat16),
            pltpu.VMEM((3,) + block, jnp.bfloat16),
            pltpu.VMEM((3,) + block, jnp.bfloat16),
            pltpu.VMEM(block, jnp.bfloat16),
            pltpu.VMEM(block, jnp.bfloat16),
            pltpu.VMEM((PER_PATCH, TILE_TOKENS, 2 * HEAD_DIM), jnp.float32),
            pltpu.VMEM(block, jnp.bfloat16),
            pltpu.SemaphoreType.DMA((5, heads)),
            pltpu.SemaphoreType.DMA((5, heads)),
            pltpu.SemaphoreType.DMA((2, 3, heads)),
            pltpu.SemaphoreType.DMA((2, 3, heads)),
            pltpu.SemaphoreType.DMA((heads,)),
            pltpu.SemaphoreType.DMA((heads,)),
        ],
        compiler_params=pltpu.CompilerParams(
            collective_id=0, has_side_effects=True, vmem_limit_bytes=48 * 1024 * 1024
        ),
        cost_estimate=pl.CostEstimate(
            flops=4 * HEAD_DIM * pairs,
            bytes_accessed=12 * query.size,
            transcendentals=2 * pairs,
        ),
        name="tile_attention",
    )(bias, query, fresh_key, fresh_value, stale_key, stale_value)


def solution(mesh):
    split = P(("cfg", "patch", "seq"), None)
    return jax.shard_map(
        on_device,
        mesh=mesh,
        in_specs=(split, split, split, split, split, P("patch", None), P("patch")),
        out_specs=split,
        check_vma=False,
    )
```

```python
import functools
import math

import jax
import jax.numpy as jnp
from jax import lax
from jax.experimental import pallas as pl
from jax.experimental.pallas import tpu as pltpu
from jax.sharding import PartitionSpec as P

NUM_HEADS = 16
HEAD_DIM = 128
TILE_TOKENS = 384
TILES_H = 2
TILES_W = 3
KEY_SLOTS = 18
PER_PATCH = TILES_H * TILES_W

SOFT_CAP = 8.0
LOG2E = math.log2(math.e)
SCORE_SCALE = 1.0 / (SOFT_CAP * HEAD_DIM**0.5)
EXP_SCALE = SOFT_CAP * LOG2E
UNUSED = 1e30

MESH = pl.DeviceIdType.MESH
BEFORE, OWN, AFTER = 0, 1, 2
STALE, CURRENT = (0, 1), (2, 3, 4)


def kernel(
    seq_count, patch_count, rows, bias, query, fresh_key, fresh_value, stale_key, stale_value, out,
    q_buf, k_buf, v_buf, ks_buf, vs_buf, acc, o_buf,
    send_in, recv_in, send_z, recv_z, send_o, recv_o,
):
    heads = NUM_HEADS // seq_count
    row_devices = seq_count // TILES_H
    me = lax.axis_index("seq")
    patch = lax.axis_index("patch")
    has_before = patch > 0
    has_after = patch < patch_count - 1

    def peer_of(step):
        return lax.rem(me + step, seq_count)

    def columns(device, head):
        return pl.ds(pl.multiple_of((device * heads + head) * HEAD_DIM, HEAD_DIM), HEAD_DIM)

    def rows_of(device):
        return pl.ds(pl.multiple_of(device * rows, 16), rows)

    barrier = pltpu.get_barrier_semaphore()
    for step in range(1, seq_count):
        pl.semaphore_signal(barrier, inc=1, device_id={"seq": peer_of(step)}, device_id_type=MESH)

    @pl.when(has_before)
    def _():
        pl.semaphore_signal(barrier, inc=1, device_id={"patch": patch - 1}, device_id_type=MESH)

    @pl.when(has_after)
    def _():
        pl.semaphore_signal(barrier, inc=1, device_id={"patch": patch + 1}, device_id_type=MESH)

    around = jnp.minimum(patch, 1) + jnp.minimum(patch_count - 1 - patch, 1)
    pl.semaphore_wait(barrier, seq_count - 1 + around)

    sources = (stale_key, stale_value, query, fresh_key, fresh_value)

    def landing(array, head):
        return (
            ks_buf.at[head], vs_buf.at[head], q_buf.at[head], k_buf.at[OWN, head], v_buf.at[OWN, head]
        )[array]

    def send_inputs(arrays, head):
        for array in arrays:
            source = sources[array]
            for step in range(1, seq_count):
                peer = peer_of(step)
                pltpu.make_async_remote_copy(
                    src_ref=source.at[:, columns(peer, head)],
                    dst_ref=landing(array, head).at[rows_of(me)],
                    send_sem=send_in.at[array, head],
                    recv_sem=recv_in.at[array, head],
                    device_id={"seq": peer},
                    device_id_type=MESH,
                ).start()
            pltpu.make_async_copy(
                source.at[:, columns(me, head)],
                landing(array, head).at[rows_of(me)],
                recv_in.at[array, head],
            ).start()

    def wait_inputs(arrays, head):
        for array in arrays:
            whole = landing(array, head)
            pltpu.make_async_copy(whole, whole, recv_in.at[array, head]).wait()

    def halo_copy(array, side, head):
        source = (ks_buf, vs_buf)[array]
        target = (k_buf, v_buf)[array]
        return pltpu.make_async_remote_copy(
            src_ref=source.at[head],
            dst_ref=target.at[side, head],
            send_sem=send_z.at[array, side, head],
            recv_sem=recv_z.at[array, side, head],
            device_id={"patch": patch + 1 if side == BEFORE else patch - 1},
            device_id_type=MESH,
        )

    def send_halo(head):
        wait_inputs(STALE, head)
        for array in STALE:

            @pl.when(has_after)
            def _():
                halo_copy(array, BEFORE, head).start()

            @pl.when(has_before)
            def _():
                halo_copy(array, AFTER, head).start()

    def attend(head, side, row):
        ones = jnp.ones((2 * TILE_TOKENS, HEAD_DIM), jnp.bfloat16)
        steps = [
            (col, first)
            for col in range(TILES_W)
            for first in ((0, 2, 4) if col == 1 else (min(col, 1), TILES_W + min(col, 1)))
        ]

        def scores_of(col, first):
            start = (row * TILES_W + col) * TILE_TOKENS
            query_rows = q_buf[head, pl.ds(pl.multiple_of(start, TILE_TOKENS), TILE_TOKENS), :]
            return lax.dot_general(
                query_rows, k_buf[side, head, pl.ds(first * TILE_TOKENS, 2 * TILE_TOKENS), :],
                (((1,), (1,)), ((), ())), preferred_element_type=jnp.float32,
            )

        ahead = scores_of(*steps[0])
        partial = None
        for index, (col, first) in enumerate(steps):
            tile = row * TILES_W + col
            scores = ahead
            if index + 1 < len(steps):
                ahead = scores_of(*steps[index + 1])
            weights = []
            for part in range(2):
                shift = bias[tile, side * PER_PATCH + first + part]
                part_scores = scores[:, part * TILE_TOKENS : (part + 1) * TILE_TOKENS]
                weight = jnp.exp2(EXP_SCALE * jnp.tanh(part_scores * SCORE_SCALE) - shift)
                weights.append(weight.astype(jnp.bfloat16))
            at = pl.ds(first * TILE_TOKENS, 2 * TILE_TOKENS)
            values = jnp.concatenate([v_buf[side, head, at, :], ones], axis=1)
            term = jnp.dot(
                jnp.concatenate(weights, axis=1), values, preferred_element_type=jnp.float32
            )
            partial = term if partial is None else partial + term
            if index + 1 == len(steps) or steps[index + 1][0] != col:
                acc[tile] += partial
                partial = None

    def send_output(head, row):
        for step in range(1, seq_count):
            peer = peer_of(step)

            @pl.when(lax.div(peer, row_devices) == row)
            def _():
                pltpu.make_async_remote_copy(
                    src_ref=o_buf.at[head, rows_of(peer)],
                    dst_ref=out.at[:, columns(me, head)],
                    send_sem=send_o.at[head],
                    recv_sem=recv_o.at[head],
                    device_id={"seq": peer},
                    device_id_type=MESH,
                ).start()

        @pl.when(lax.div(me, row_devices) == row)
        def _():
            pltpu.make_async_copy(
                o_buf.at[head, rows_of(me)], out.at[:, columns(me, head)], recv_o.at[head]
            ).start()

    for head in range(min(2, heads)):
        send_inputs(STALE, head)
    send_halo(0)
    send_inputs(CURRENT, 0)
    if heads > 1:
        send_halo(1)
    if heads > 2:
        send_inputs(STALE, 2)

    def wait_halo(side, head):
        for array, target in enumerate((k_buf, v_buf)):
            whole = target.at[side, head]
            pltpu.make_async_copy(whole, whole, recv_z.at[array, side, head]).wait()

    def head_step(head, carry):
        acc[...] = jnp.zeros_like(acc)
        wait_inputs((2,), head)

        @pl.when(head + 1 < heads)
        def _():
            send_inputs(CURRENT, head + 1)

        def near_step(index, carry):
            side = 2 * index
            other = patch - 1 + side

            @pl.when(jnp.logical_and(other >= 0, other < patch_count))
            def _():
                wait_halo(side, head)

                def row_step(row, carry):
                    attend(head, side, row)
                    return carry

                lax.fori_loop(0, TILES_H, row_step, 0)

            return carry

        lax.fori_loop(0, 2, near_step, 0)
        wait_inputs((3, 4), head)

        @pl.when(head > 0)
        def _():
            for row in range(TILES_H):
                send_output(head - 1, row)

        def own_step(row, carry):
            attend(head, OWN, row)
            for col in range(TILES_W):
                tile = row * TILES_W + col
                tile_rows = pl.ds(pl.multiple_of(tile * TILE_TOKENS, TILE_TOKENS), TILE_TOKENS)
                o_buf[head, tile_rows, :] = (
                    acc[tile, :, :HEAD_DIM] / acc[tile, :, HEAD_DIM:]
                ).astype(jnp.bfloat16)

            @pl.when(head == heads - 1)
            def _():
                send_output(head, row)

            return carry

        lax.fori_loop(0, TILES_H, own_step, 0)

        @pl.when(head + 2 < heads)
        def _():
            send_halo(head + 2)

        @pl.when(head + 3 < heads)
        def _():
            send_inputs(STALE, head + 3)

        return carry

    lax.fori_loop(0, heads, head_step, 0)

    sent = pl.ds(0, (seq_count - 1) * rows)
    for head in range(heads):
        for array in range(len(sources)):
            part = landing(array, head).at[sent]
            pltpu.make_async_copy(part, part, send_in.at[array, head]).wait()
        for array in STALE:

            @pl.when(has_after)
            def _():
                halo_copy(array, BEFORE, head).wait_send()

            @pl.when(has_before)
            def _():
                halo_copy(array, AFTER, head).wait_send()

        part = o_buf.at[head, sent]
        pltpu.make_async_copy(part, part, send_o.at[head]).wait()
        whole = o_buf.at[head]
        pltpu.make_async_copy(whole, whole, recv_o.at[head]).wait()


def on_device(query, fresh_key, fresh_value, stale_key, stale_value, key_tiles, tile_count):
    seq_count = lax.axis_size("seq")
    patch_count = lax.axis_size("patch")
    heads = NUM_HEADS // seq_count
    rows = query.shape[0]
    patch_rows = rows * seq_count
    first_tile = (lax.axis_index("patch") - 1) * PER_PATCH
    used = jnp.arange(KEY_SLOTS, dtype=jnp.int32)[None, :] < tile_count[:, None]
    near = jnp.arange(3 * PER_PATCH, dtype=jnp.int32)
    listed = jnp.any(
        used[:, :, None] & ((key_tiles - first_tile)[:, :, None] == near[None, None, :]), axis=1
    )
    bias = jnp.where(listed, EXP_SCALE, UNUSED).astype(jnp.float32)
    block = (heads, patch_rows, HEAD_DIM)
    pairs = patch_rows * TILES_H * 7 * TILE_TOKENS * 3 * heads // TILES_W
    return pl.pallas_call(
        functools.partial(kernel, seq_count, patch_count, rows),
        out_shape=jax.ShapeDtypeStruct(query.shape, jnp.bfloat16),
        in_specs=[pl.BlockSpec(memory_space=pltpu.SMEM)] + [pl.BlockSpec(memory_space=pl.ANY)] * 5,
        out_specs=pl.BlockSpec(memory_space=pl.ANY),
        scratch_shapes=[
            pltpu.VMEM(block, jnp.bfloat16),
            pltpu.VMEM((3,) + block, jnp.bfloat16),
            pltpu.VMEM((3,) + block, jnp.bfloat16),
            pltpu.VMEM(block, jnp.bfloat16),
            pltpu.VMEM(block, jnp.bfloat16),
            pltpu.VMEM((PER_PATCH, TILE_TOKENS, 2 * HEAD_DIM), jnp.float32),
            pltpu.VMEM(block, jnp.bfloat16),
            pltpu.SemaphoreType.DMA((5, heads)),
            pltpu.SemaphoreType.DMA((5, heads)),
            pltpu.SemaphoreType.DMA((2, 3, heads)),
            pltpu.SemaphoreType.DMA((2, 3, heads)),
            pltpu.SemaphoreType.DMA((heads,)),
            pltpu.SemaphoreType.DMA((heads,)),
        ],
        compiler_params=pltpu.CompilerParams(
            collective_id=0, has_side_effects=True, vmem_limit_bytes=62 * 1024 * 1024
        ),
        cost_estimate=pl.CostEstimate(
            flops=4 * HEAD_DIM * pairs,
            bytes_accessed=12 * query.size,
            transcendentals=2 * pairs,
        ),
        name="tile_attention",
    )(bias, query, fresh_key, fresh_value, stale_key, stale_value)


def solution(mesh):
    split = P(("cfg", "patch", "seq"), None)
    return jax.shard_map(
        on_device,
        mesh=mesh,
        in_specs=(split, split, split, split, split, P("patch", None), P("patch")),
        out_specs=split,
        check_vma=False,
    )
```

```python
import functools
import math

import jax
import jax.numpy as jnp
from jax import lax
from jax.experimental import pallas as pl
from jax.experimental.pallas import tpu as pltpu
from jax.sharding import PartitionSpec as P

NUM_HEADS = 16
HEAD_DIM = 128
TILE_TOKENS = 384
TILES_H = 2
TILES_W = 3
KEY_SLOTS = 18
PER_PATCH = TILES_H * TILES_W

SOFT_CAP = 8.0
LOG2E = math.log2(math.e)
SCORE_SCALE = 1.0 / (SOFT_CAP * HEAD_DIM**0.5)
EXP_SCALE = SOFT_CAP * LOG2E
UNUSED = 1e30

MESH = pl.DeviceIdType.MESH
BEFORE, OWN, AFTER = 0, 1, 2
STALE, CURRENT = (0, 1), (2, 3, 4)


def kernel(
    seq_count, patch_count, rows, bias, query, fresh_key, fresh_value, stale_key, stale_value, out,
    q_buf, k_buf, v_buf, ks_buf, vs_buf, acc, o_buf, w_buf,
    send_in, recv_in, send_z, recv_z, send_o, recv_o,
):
    heads = NUM_HEADS // seq_count
    row_devices = seq_count // TILES_H
    me = lax.axis_index("seq")
    patch = lax.axis_index("patch")
    has_before = patch > 0
    has_after = patch < patch_count - 1

    def peer_of(step):
        return lax.rem(me + step, seq_count)

    def columns(device, head):
        return pl.ds(pl.multiple_of((device * heads + head) * HEAD_DIM, HEAD_DIM), HEAD_DIM)

    def rows_of(device):
        return pl.ds(pl.multiple_of(device * rows, 16), rows)

    barrier = pltpu.get_barrier_semaphore()
    for step in range(1, seq_count):
        pl.semaphore_signal(barrier, inc=1, device_id={"seq": peer_of(step)}, device_id_type=MESH)

    @pl.when(has_before)
    def _():
        pl.semaphore_signal(barrier, inc=1, device_id={"patch": patch - 1}, device_id_type=MESH)

    @pl.when(has_after)
    def _():
        pl.semaphore_signal(barrier, inc=1, device_id={"patch": patch + 1}, device_id_type=MESH)

    around = jnp.minimum(patch, 1) + jnp.minimum(patch_count - 1 - patch, 1)
    pl.semaphore_wait(barrier, seq_count - 1 + around)

    sources = (stale_key, stale_value, query, fresh_key, fresh_value)

    def landing(array, head):
        return (
            ks_buf.at[head], vs_buf.at[head], q_buf.at[head], k_buf.at[OWN, head], v_buf.at[OWN, head]
        )[array]

    def send_inputs(arrays, head):
        for array in arrays:
            source = sources[array]
            for step in range(1, seq_count):
                peer = peer_of(step)
                pltpu.make_async_remote_copy(
                    src_ref=source.at[:, columns(peer, head)],
                    dst_ref=landing(array, head).at[rows_of(me)],
                    send_sem=send_in.at[array, head],
                    recv_sem=recv_in.at[array, head],
                    device_id={"seq": peer},
                    device_id_type=MESH,
                ).start()
            pltpu.make_async_copy(
                source.at[:, columns(me, head)],
                landing(array, head).at[rows_of(me)],
                recv_in.at[array, head],
            ).start()

    def wait_inputs(arrays, head):
        for array in arrays:
            whole = landing(array, head)
            pltpu.make_async_copy(whole, whole, recv_in.at[array, head]).wait()

    def halo_copy(array, side, head):
        source = (ks_buf, vs_buf)[array]
        target = (k_buf, v_buf)[array]
        return pltpu.make_async_remote_copy(
            src_ref=source.at[head],
            dst_ref=target.at[side, head],
            send_sem=send_z.at[array, side, head],
            recv_sem=recv_z.at[array, side, head],
            device_id={"patch": patch + 1 if side == BEFORE else patch - 1},
            device_id_type=MESH,
        )

    def send_halo(head):
        wait_inputs(STALE, head)
        for array in STALE:

            @pl.when(has_after)
            def _():
                halo_copy(array, BEFORE, head).start()

            @pl.when(has_before)
            def _():
                halo_copy(array, AFTER, head).start()

    def attend(head, side, row, phase):
        ones = jnp.ones((2 * TILE_TOKENS, HEAD_DIM), jnp.bfloat16)
        steps = [
            (col, first)
            for col in range(TILES_W)
            for first in ((0, 2, 4) if col == 1 else (min(col, 1), TILES_W + min(col, 1)))
        ]

        def scores_of(col, first):
            start = (row * TILES_W + col) * TILE_TOKENS
            query_rows = q_buf[head, pl.ds(pl.multiple_of(start, TILE_TOKENS), TILE_TOKENS), :]
            return lax.dot_general(
                query_rows, k_buf[side, head, pl.ds(first * TILE_TOKENS, 2 * TILE_TOKENS), :],
                (((1,), (1,)), ((), ())), preferred_element_type=jnp.float32,
            )

        def weights_of(scores, col, first):
            weights = []
            for part in range(2):
                shift = bias[row * TILES_W + col, side * PER_PATCH + first + part]
                part_scores = scores[:, part * TILE_TOKENS : (part + 1) * TILE_TOKENS]
                weight = jnp.exp2(EXP_SCALE * jnp.tanh(part_scores * SCORE_SCALE) - shift)
                weights.append(weight.astype(jnp.bfloat16))
            return jnp.concatenate(weights, axis=1)

        if phase != "values":
            ahead = scores_of(*steps[0])
        partial = None
        for index, (col, first) in enumerate(steps):
            if phase == "values":
                weights = w_buf[row, index]
            else:
                scores = ahead
                if index + 1 < len(steps):
                    ahead = scores_of(*steps[index + 1])
                weights = weights_of(scores, col, first)
            if phase == "weights":
                w_buf[row, index] = weights
                continue
            at = pl.ds(first * TILE_TOKENS, 2 * TILE_TOKENS)
            values = jnp.concatenate([v_buf[side, head, at, :], ones], axis=1)
            term = jnp.dot(weights, values, preferred_element_type=jnp.float32)
            partial = term if partial is None else partial + term
            if index + 1 == len(steps) or steps[index + 1][0] != col:
                acc[row * TILES_W + col] += partial
                partial = None

    def send_output(head, row):
        for step in range(1, seq_count):
            peer = peer_of(step)

            @pl.when(lax.div(peer, row_devices) == row)
            def _():
                pltpu.make_async_remote_copy(
                    src_ref=o_buf.at[head, rows_of(peer)],
                    dst_ref=out.at[:, columns(me, head)],
                    send_sem=send_o.at[head],
                    recv_sem=recv_o.at[head],
                    device_id={"seq": peer},
                    device_id_type=MESH,
                ).start()

        @pl.when(lax.div(me, row_devices) == row)
        def _():
            pltpu.make_async_copy(
                o_buf.at[head, rows_of(me)], out.at[:, columns(me, head)], recv_o.at[head]
            ).start()

    for head in range(min(2, heads)):
        send_inputs(STALE, head)
    send_halo(0)
    send_inputs(CURRENT, 0)
    if heads > 1:
        send_halo(1)
    if heads > 2:
        send_inputs(STALE, 2)

    def wait_halo(side, head):
        for array, target in enumerate((k_buf, v_buf)):
            whole = target.at[side, head]
            pltpu.make_async_copy(whole, whole, recv_z.at[array, side, head]).wait()

    def head_step(head, carry):
        acc[...] = jnp.zeros_like(acc)
        wait_inputs((2,), head)

        @pl.when(head + 1 < heads)
        def _():
            send_inputs(CURRENT, head + 1)

        def near_step(index, carry):
            side = 2 * index
            other = patch - 1 + side

            @pl.when(jnp.logical_and(other >= 0, other < patch_count))
            def _():
                wait_halo(side, head)

                def row_step(row, carry):
                    attend(head, side, row, "both")
                    return carry

                lax.fori_loop(0, TILES_H, row_step, 0)

            return carry

        lax.fori_loop(0, 2, near_step, 0)
        wait_inputs((3,), head)

        def weight_step(row, carry):
            attend(head, OWN, row, "weights")
            return carry

        lax.fori_loop(0, TILES_H, weight_step, 0)
        wait_inputs((4,), head)

        @pl.when(head > 0)
        def _():
            for row in range(TILES_H):
                send_output(head - 1, row)

        def own_step(row, carry):
            attend(head, OWN, row, "values")
            for col in range(TILES_W):
                tile = row * TILES_W + col
                tile_rows = pl.ds(pl.multiple_of(tile * TILE_TOKENS, TILE_TOKENS), TILE_TOKENS)
                o_buf[head, tile_rows, :] = (
                    acc[tile, :, :HEAD_DIM] / acc[tile, :, HEAD_DIM:]
                ).astype(jnp.bfloat16)

            @pl.when(head == heads - 1)
            def _():
                send_output(head, row)

            return carry

        lax.fori_loop(0, TILES_H, own_step, 0)

        @pl.when(head + 2 < heads)
        def _():
            send_halo(head + 2)

        @pl.when(head + 3 < heads)
        def _():
            send_inputs(STALE, head + 3)

        return carry

    lax.fori_loop(0, heads, head_step, 0)

    sent = pl.ds(0, (seq_count - 1) * rows)
    for head in range(heads):
        for array in range(len(sources)):
            part = landing(array, head).at[sent]
            pltpu.make_async_copy(part, part, send_in.at[array, head]).wait()
        for array in STALE:

            @pl.when(has_after)
            def _():
                halo_copy(array, BEFORE, head).wait_send()

            @pl.when(has_before)
            def _():
                halo_copy(array, AFTER, head).wait_send()

        part = o_buf.at[head, sent]
        pltpu.make_async_copy(part, part, send_o.at[head]).wait()
        whole = o_buf.at[head]
        pltpu.make_async_copy(whole, whole, recv_o.at[head]).wait()


def on_device(query, fresh_key, fresh_value, stale_key, stale_value, key_tiles, tile_count):
    seq_count = lax.axis_size("seq")
    patch_count = lax.axis_size("patch")
    heads = NUM_HEADS // seq_count
    rows = query.shape[0]
    patch_rows = rows * seq_count
    first_tile = (lax.axis_index("patch") - 1) * PER_PATCH
    used = jnp.arange(KEY_SLOTS, dtype=jnp.int32)[None, :] < tile_count[:, None]
    near = jnp.arange(3 * PER_PATCH, dtype=jnp.int32)
    listed = jnp.any(
        used[:, :, None] & ((key_tiles - first_tile)[:, :, None] == near[None, None, :]), axis=1
    )
    bias = jnp.where(listed, EXP_SCALE, UNUSED).astype(jnp.float32)
    block = (heads, patch_rows, HEAD_DIM)
    pairs = patch_rows * TILES_H * 7 * TILE_TOKENS * 3 * heads // TILES_W
    return pl.pallas_call(
        functools.partial(kernel, seq_count, patch_count, rows),
        out_shape=jax.ShapeDtypeStruct(query.shape, jnp.bfloat16),
        in_specs=[pl.BlockSpec(memory_space=pltpu.SMEM)] + [pl.BlockSpec(memory_space=pl.ANY)] * 5,
        out_specs=pl.BlockSpec(memory_space=pl.ANY),
        scratch_shapes=[
            pltpu.VMEM(block, jnp.bfloat16),
            pltpu.VMEM((3,) + block, jnp.bfloat16),
            pltpu.VMEM((3,) + block, jnp.bfloat16),
            pltpu.VMEM(block, jnp.bfloat16),
            pltpu.VMEM(block, jnp.bfloat16),
            pltpu.VMEM((PER_PATCH, TILE_TOKENS, 2 * HEAD_DIM), jnp.float32),
            pltpu.VMEM(block, jnp.bfloat16),
            pltpu.VMEM((TILES_H, 7, TILE_TOKENS, 2 * TILE_TOKENS), jnp.bfloat16),
            pltpu.SemaphoreType.DMA((5, heads)),
            pltpu.SemaphoreType.DMA((5, heads)),
            pltpu.SemaphoreType.DMA((2, 3, heads)),
            pltpu.SemaphoreType.DMA((2, 3, heads)),
            pltpu.SemaphoreType.DMA((heads,)),
            pltpu.SemaphoreType.DMA((heads,)),
        ],
        compiler_params=pltpu.CompilerParams(
            collective_id=0, has_side_effects=True, vmem_limit_bytes=48 * 1024 * 1024
        ),
        cost_estimate=pl.CostEstimate(
            flops=4 * HEAD_DIM * pairs,
            bytes_accessed=12 * query.size,
            transcendentals=2 * pairs,
        ),
        name="tile_attention",
    )(bias, query, fresh_key, fresh_value, stale_key, stale_value)


def solution(mesh):
    split = P(("cfg", "patch", "seq"), None)
    return jax.shard_map(
        on_device,
        mesh=mesh,
        in_specs=(split, split, split, split, split, P("patch", None), P("patch")),
        out_specs=split,
        check_vma=False,
    )
```
